512 devices in a mesh: slab: 64 (over y, x, z_hi, core), head: 8 (over z_lo).
Axes of the slice: x: 4, y: 4, z: 16 (z_hi: 2, z_lo: 8; z = z_hi * 8 + z_lo), core: 2. Of those that a mesh axis runs over, the one named last changes fastest.
Arguments:
- fresh_qkv: bfloat16 [3, 8192, 3072], P(None, ('slab', 'head')), may hold values from -6 to 6
- stale_kv: bfloat16 [2, 8192, 3072], P(None, 'slab', 'head'), may hold values from -6 to 6
- out_weight: bfloat16 [3072, 3072], P('head'), may hold values from -0.109375 to 0.109375
- branch_gate: float32 [3072], replicated, may hold values from 0.5 to 2
- residual: bfloat16 [8192, 3072], P(('slab', 'head')), may hold values from -6 to 6
Outputs:
- block_out: bfloat16 [8192, 3072], P(('slab', 'head'))
- next_kv: bfloat16 [2, 8192, 3072], P(None, 'slab', 'head')
The draws below stay inside these ranges and needn't reach their ends.
All inputs are finite; a program needn't handle non-finite values.
Results may differ from the reference program's by a relative error of at most 0.014.
Values may be sent and summed in bfloat16 or wider, within the bound.
No kernel may reach another device: no remote copies, remote signals or barrier semaphores. Data moves between devices by JAX's collectives and lax.ppermute only.
A program may use at most 64 MiB of HBM per device.

```python
import math
import jax
import jax.numpy as jnp
from jax import lax

HEADS = 24
HEAD_DIM = 128
D = 3072
SLAB = 128
TOKENS = 8192
N_SLAB = 64


def draw_fresh_qkv(key, part):
    key = jax.random.fold_in(key, 11)
    drawn_key = jax.random.fold_in(key, 0)
    spread = 1.58
    drawn = jax.random.normal(drawn_key, (3, TOKENS, D), jnp.float32) * spread
    result = jnp.clip(drawn, -6.0, 6.0)
    return result.astype(jnp.bfloat16)


def steps_of(key, extent, cuts, low, top_value):
    loudness = 1.0
    for position, parts in cuts:
        heights = jax.random.uniform(jax.random.fold_in(jax.random.fold_in(key, 6), position), (parts,), jnp.float32, low / len(cuts), top_value / len(cuts))
        loudness = loudness * jnp.repeat(jnp.exp(heights), extent[position] // parts).reshape((-1,) + (1,) * (len(extent) - 1 - position))
    return loudness


def gaussian(key, shape, scale, most, cuts=(), kind=jnp.bfloat16):
    values = scale * jax.random.normal(key, shape, jnp.float32)
    if cuts:
        values = values * steps_of(key, shape, cuts, -0.22, 0.18)
    return jnp.clip(values, -most, most).astype(kind)


def setup_inputs(seed: int = 0) -> dict:
    key_of = jax.random.split(jax.random.key(seed), 6)
    fresh_qkv = draw_fresh_qkv(jax.random.fold_in(key_of[5], 71), 0)
    stale_kv = gaussian(key_of[1], (2, TOKENS, D), 1.58, 6.0, ((1, 64), (2, 8)))
    out_weight = gaussian(key_of[2], (D, D), D ** -0.5, 0.109375, ((0, 8),))
    branch_gate = jnp.clip(jax.random.uniform(key_of[3], (D,), jnp.float32, 0.5, 2.0), 0.5, 2.0)
    residual = gaussian(key_of[4], (TOKENS, D), 1.0, 6.0, ((0, 512),))
    return dict(fresh_qkv=fresh_qkv, stale_kv=stale_kv, out_weight=out_weight, branch_gate=branch_gate, residual=residual)


def reference(fresh_qkv, stale_kv, out_weight, branch_gate, residual):
    score_scale = 1.0 / math.sqrt(HEAD_DIM)
    stale_keys = stale_kv[0].astype(jnp.float32).reshape(TOKENS, HEADS, HEAD_DIM)
    stale_values = stale_kv[1].astype(jnp.float32).reshape(TOKENS, HEADS, HEAD_DIM)

    def one_slab(slab_no):
        first = (slab_no * SLAB).astype(jnp.int32)
        slab_block = lax.dynamic_slice_in_dim(fresh_qkv, first, SLAB, 1).astype(jnp.float32)
        queries = slab_block[0].reshape(SLAB, HEADS, HEAD_DIM)
        own_keys = slab_block[1].reshape(SLAB, HEADS, HEAD_DIM)
        own_values = slab_block[2].reshape(SLAB, HEADS, HEAD_DIM)
        scores = jnp.einsum('qhd,khd->hqk', queries, stale_keys) * score_scale
        own_scores = jnp.einsum('qhd,khd->hqk', queries, own_keys) * score_scale
        zero = jnp.zeros((), jnp.int32)
        scores = lax.dynamic_update_slice(scores, own_scores, (zero, zero, first))
        all_values = lax.dynamic_update_slice(stale_values, own_values, (first, zero, zero))
        row_top = lax.optimization_barrier(jnp.max(scores, axis=2, keepdims=True))
        expd = jnp.exp(scores - row_top)
        row_total = lax.optimization_barrier(jnp.sum(expd, axis=2))
        weights = expd.astype(jnp.bfloat16).astype(jnp.float32)
        summed = jnp.einsum('hqk,khd->qhd', weights, all_values)
        attended = summed / jnp.transpose(row_total)[:, :, None]
        return attended.astype(jnp.bfloat16).reshape(SLAB, D)
    attended = lax.map(one_slab, jnp.arange(N_SLAB, dtype=jnp.int32)).reshape(TOKENS, D)
    projected = jnp.dot(attended, out_weight, preferred_element_type=jnp.float32)
    block_out = (residual.astype(jnp.float32) + branch_gate[None, :] * projected).astype(jnp.bfloat16)
    next_kv = fresh_qkv[1:3]
    return (block_out, next_kv)
```

```python
import functools
import math

import jax
import jax.numpy as jnp
from jax import lax
from jax.experimental import pallas as pl
from jax.experimental.pallas import tpu as pltpu
from jax.sharding import Mesh, PartitionSpec as P

HEAD_DIM = 128
AXES = ("yh", "yl", "x", "zh", "core", "head")
SLAB_AXES = AXES[:-1]
SIZES = (2, 2, 4, 2, 2, 8)
KEY_AXES = ("yh", "x")
N_HEAD = 8
HEADS_HERE = 3
WIDTH = HEADS_HERE * HEAD_DIM
SLAB = 128
PIECE = SLAB // N_HEAD
D = N_HEAD * WIDTH
KEY_SLABS = 8
KEYS = KEY_SLABS * SLAB
PAIR = 2 * SLAB
STAT_ROWS = 16
ROWS = WIDTH + STAT_ROWS
LOG2E = 1.4426950408889634
FACTOR = LOG2E / math.sqrt(HEAD_DIM)
MASKED = -1e30
PIECE_ORDER = (0, 4, 2, 6, 1, 5, 3, 7)

VMEM = pl.BlockSpec(memory_space=pltpu.VMEM)
SMEM = pl.BlockSpec(memory_space=pltpu.SMEM)
ANY = pl.BlockSpec(memory_space=pl.ANY)
BF16 = jnp.bfloat16
F32 = jnp.float32


def swap(n, bit):
    return [(i, i ^ bit) for i in range(n)]


def call(body, out_shape, n_in, scratch=(), in_specs=None, flops=0, vmem=None, name=None):
    out_specs = jax.tree.map(lambda _: VMEM, out_shape)
    return pl.pallas_call(
        body,
        out_shape=out_shape,
        in_specs=in_specs or [VMEM] * n_in,
        out_specs=out_specs,
        scratch_shapes=list(scratch),
        compiler_params=pltpu.CompilerParams(vmem_limit_bytes=vmem or (32 << 20)),
        cost_estimate=pl.CostEstimate(flops=flops, bytes_accessed=1 << 19, transcendentals=0),
        name=name,
    )


def shape(dims, dtype):
    return jax.ShapeDtypeStruct(dims, dtype)


def pack_q_body(fresh_ref, out_ref):
    for h in range(N_HEAD):
        piece = fresh_ref[0, :, h * WIDTH : (h + 1) * WIDTH]
        out_ref[h] = piece
        out_ref[N_HEAD + h] = piece


def pack_kv_body(fresh_ref, after_ref, out_ref):
    del after_ref
    for h in range(N_HEAD):
        for part in range(2):
            out_ref[h, part] = fresh_ref[1 + part, :, h * WIDTH : (h + 1) * WIDTH]


def stat_rows(lses):
    n = lses[0].shape[1]
    high = [v.astype(BF16).astype(F32) for v in lses]
    rest = [v - w for v, w in zip(lses, high)]
    mid = [v.astype(BF16).astype(F32) for v in rest]
    low = [v - w for v, w in zip(rest, mid)]
    pad = jnp.zeros((STAT_ROWS - 3 * HEADS_HERE, n), F32)
    return jnp.concatenate(high + mid + low + [pad], axis=0).astype(BF16)


def read_stats(rows):
    rows = rows.astype(F32)
    n = HEADS_HERE
    return [rows[h : h + 1] + rows[n + h : n + h + 1] + rows[2 * n + h : 2 * n + h + 1] for h in range(n)]


def soft(s, values_t):
    top = jnp.max(s, axis=0, keepdims=True)
    weights = jnp.exp2((s - top) * FACTOR)
    total = jnp.sum(weights, axis=0, keepdims=True)
    summed = jnp.dot(values_t, weights.astype(BF16), preferred_element_type=F32)
    return summed / total, top * FACTOR + jnp.log2(total)


def scores_of(keys, queries):
    return lax.dot_general(keys, queries, (((1,), (1,)), ((), ())), preferred_element_type=F32)


def attend_body(own_first, pos_ref, qa_ref, qb_ref, kv_ref, oa_ref, ob_ref, s_ref):
    lses = [[], []]
    for h in range(HEADS_HERE):
        cols = slice(h * HEAD_DIM, (h + 1) * HEAD_DIM)
        keys = kv_ref[:, 0, :, cols].reshape(KEYS, HEAD_DIM)
        values_t = kv_ref[:, 1, :, cols].reshape(KEYS, HEAD_DIM).T
        for i, (q_ref, o_ref) in enumerate(((qa_ref, oa_ref), (qb_ref, ob_ref))):
            s_ref[i] = scores_of(keys, q_ref[:, cols])
            if own_first and i == 0:
                first = pl.multiple_of(pos_ref[0] * SLAB, SLAB)
                lane = pl.multiple_of(pos_ref[1] * SLAB, SLAB)
                s_ref[0, pl.ds(first, SLAB), pl.ds(lane, SLAB)] = jnp.full((SLAB, SLAB), MASKED, F32)
            out, lse = soft(s_ref[i], values_t)
            o_ref[h * HEAD_DIM : (h + 1) * HEAD_DIM] = out.astype(BF16)
            lses[i].append(lse)
    oa_ref[WIDTH:] = stat_rows(lses[0])
    ob_ref[WIDTH:] = stat_rows(lses[1])


def attend(own_first, pos, qa, qb, kv):
    return call(
        functools.partial(attend_body, own_first),
        (shape((ROWS, PAIR), BF16), shape((ROWS, PAIR), BF16)),
        4,
        scratch=[pltpu.VMEM((2, KEYS, PAIR), F32)],
        in_specs=[SMEM, VMEM, VMEM, VMEM],
        flops=4 * HEADS_HERE * KEYS * 2 * PAIR * HEAD_DIM,
        name="attend",
    )(pos, qa, qb, kv)


def own_body(pos_ref, q_ref, fresh_ref, out_ref, next_ref):
    for piece in range(N_HEAD):
        for part in range(2):
            next_ref[part, piece * PIECE : (piece + 1) * PIECE] = fresh_ref[piece, part]
    row = pl.multiple_of(pos_ref[1] * SLAB, SLAB)
    lses = []
    for h in range(HEADS_HERE):
        cols = slice(h * HEAD_DIM, (h + 1) * HEAD_DIM)
        s = scores_of(next_ref[0, :, cols], q_ref[pl.ds(row, SLAB), cols])
        out, lse = soft(s, next_ref[1, :, cols].T)
        out_ref[h * HEAD_DIM : (h + 1) * HEAD_DIM] = out
        lses.append(lse)
    out_ref[WIDTH:] = jnp.concatenate(lses + [jnp.zeros((8 - HEADS_HERE, SLAB), F32)], axis=0)


def merge(outs, lses):
    top = functools.reduce(jnp.maximum, lses)
    shares = [jnp.exp2(v - top) for v in lses]
    total = sum(shares)
    merged = sum(o.astype(F32) * (w / total) for o, w in zip(outs, shares))
    return merged, top + jnp.log2(total)


def merge_to_bf16(parts, out_ref):
    stats = [read_stats(p[WIDTH:]) for p in parts]
    lses = []
    for h in range(HEADS_HERE):
        rows = slice(h * HEAD_DIM, (h + 1) * HEAD_DIM)
        out, lse = merge([p[rows] for p in parts], [v[h] for v in stats])
        out_ref[rows] = out.astype(BF16)
        lses.append(lse)
    out_ref[WIDTH:] = stat_rows(lses)


def merge_two_body(a_ref, b_ref, out_ref):
    merge_to_bf16([a_ref, b_ref], out_ref)


def merge_three_body(pos_ref, a_ref, b_ref, c_ref, keep_ref, send_ref):
    here = pl.multiple_of(pos_ref[1] * SLAB, SLAB)
    there = pl.multiple_of((1 - pos_ref[1]) * SLAB, SLAB)
    refs = (a_ref, b_ref, c_ref)
    merge_to_bf16([r.at[:, pl.ds(there, SLAB)] for r in refs], send_ref)
    parts = [r.at[:, pl.ds(here, SLAB)] for r in refs]
    stats = [read_stats(p[WIDTH:]) for p in parts]
    lses = []
    for h in range(HEADS_HERE):
        rows = slice(h * HEAD_DIM, (h + 1) * HEAD_DIM)
        out, lse = merge([p[rows] for p in parts], [v[h] for v in stats])
        keep_ref[rows] = out
        lses.append(lse)
    keep_ref[WIDTH:] = jnp.concatenate(lses + [jnp.zeros((8 - HEADS_HERE, SLAB), F32)], axis=0)


def project_body(pos_ref, keep_ref, other_ref, own_ref, w_ref, keep_out, send_out, att_ref, proj_ref):
    other = read_stats(other_ref[WIDTH:])
    for h in range(HEADS_HERE):
        rows = slice(h * HEAD_DIM, (h + 1) * HEAD_DIM)
        out, _ = merge(
            [keep_ref[rows], other_ref[rows], own_ref[rows]],
            [keep_ref[WIDTH + h : WIDTH + h + 1], other[h], own_ref[WIDTH + h : WIDTH + h + 1]],
        )
        att_ref[:, rows] = out.T.astype(BF16)
    proj = jnp.dot(att_ref[...], w_ref[...], preferred_element_type=F32)
    for at, piece in enumerate(PIECE_ORDER):
        proj_ref[at * PIECE : (at + 1) * PIECE] = proj[piece * PIECE : (piece + 1) * PIECE]
    half = SLAB // 2
    bit = pos_ref[2]
    keep_out[...] = proj_ref[pl.ds(pl.multiple_of(bit * half, half), half)]
    send_out[...] = proj_ref[pl.ds(pl.multiple_of((1 - bit) * half, half), half)].astype(BF16)


def local(fresh_qkv, stale_kv, out_weight, branch_gate, residual):
    head = lax.axis_index("head")
    zh = lax.axis_index("zh")
    pos = jnp.stack([lax.axis_index(KEY_AXES), zh, head % 2]).astype(jnp.int32)

    kv = lax.all_gather(stale_kv, KEY_AXES, axis=0, tiled=False)

    q_packed = call(pack_q_body, shape((2 * N_HEAD, PIECE, WIDTH), BF16), 1, name="pack_q")(fresh_qkv[0:1])
    q_all = lax.all_to_all(q_packed, ("zh", "head"), 0, 0, tiled=True)
    q0 = q_all.reshape(PAIR, WIDTH)
    q2 = lax.ppermute(q0, "core", swap(2, 1))
    q1 = lax.ppermute(q0, "yl", swap(2, 1))
    q3 = lax.ppermute(q1, "core", swap(2, 1))

    kv_packed = call(
        pack_kv_body, shape((N_HEAD, 2, PIECE, WIDTH), BF16), 2, in_specs=[VMEM, ANY], name="pack_kv"
    )(fresh_qkv, q_all)
    kv_fresh = lax.all_to_all(kv_packed, "head", 0, 0, tiled=True)

    m0, m2 = attend(True, pos, q0, q2, kv)
    m0_core = lax.ppermute(m2, "core", swap(2, 1))
    m1, m3 = attend(False, pos, q1, q3, kv)
    m1_core = lax.ppermute(m3, "core", swap(2, 1))
    m1_sum = call(merge_two_body, shape((ROWS, PAIR), BF16), 2, name="merge_two")(m1, m1_core)
    m0_y = lax.ppermute(m1_sum, "yl", swap(2, 1))

    own, next_kv = call(
        own_body,
        (shape((WIDTH + 8, SLAB), F32), shape((2, SLAB, WIDTH), BF16)),
        3,
        in_specs=[SMEM, VMEM, VMEM],
        name="own",
    )(pos, q0, kv_fresh)

    keep, send = call(
        merge_three_body,
        (shape((WIDTH + 8, SLAB), F32), shape((ROWS, SLAB), BF16)),
        4,
        in_specs=[SMEM, VMEM, VMEM, VMEM],
        name="merge_three",
    )(pos, m0, m0_core, m0_y)
    other = lax.ppermute(send, "zh", swap(2, 1))

    kept, sent = call(
        project_body,
        (shape((SLAB // 2, D), F32), shape((SLAB // 2, D), BF16)),
        5,
        scratch=[pltpu.VMEM((SLAB, WIDTH), BF16), pltpu.VMEM((SLAB, D), F32)],
        in_specs=[SMEM] + [VMEM] * 4,
        name="project",
    )(pos, keep, other, own, out_weight)

    for bit in (1, 2, 4):
        kept = kept + lax.ppermute(sent, "head", swap(N_HEAD, bit)).astype(F32)
        if bit < 4:
            rows = kept.shape[0] // 2
            mine = (head // (2 * bit)) % 2
            sent = lax.dynamic_slice_in_dim(kept, (1 - mine) * rows, rows, 0).astype(BF16)
            kept = lax.dynamic_slice_in_dim(kept, mine * rows, rows, 0)
    block_out = (residual.astype(F32) + branch_gate[None, :] * kept).astype(BF16)
    return block_out, next_kv


def solution(mesh):
    fine = Mesh(mesh.devices.reshape(SIZES), AXES)
    return jax.shard_map(
        local,
        mesh=fine,
        in_specs=(
            P(None, AXES, None),
            P(None, SLAB_AXES, "head"),
            P("head", None),
            P(),
            P(AXES, None),
        ),
        out_specs=(P(AXES, None), P(None, SLAB_AXES, "head")),
        check_vma=False,
    )
```

```python
import functools
import math

import jax
import jax.numpy as jnp
from jax import lax
from jax.experimental import pallas as pl
from jax.experimental.pallas import tpu as pltpu
from jax.sharding import Mesh, PartitionSpec as P

HEAD_DIM = 128
AXES = ("y", "x", "zh", "core", "head")
SLAB_AXES = AXES[:-1]
SIZES = (4, 4, 2, 2, 8)
N_HEAD = 8
HEADS_HERE = 3
WIDTH = HEADS_HERE * HEAD_DIM
SLAB = 128
PIECE = SLAB // N_HEAD
D = N_HEAD * WIDTH
KEY_SLABS = 8
KEYS = KEY_SLABS * SLAB
PAIR = 2 * SLAB
QUERY_SLABS = 4
QUERY_FROM = (0, 1, 3, 2)
PARTS = 2
LONG = 40_000_000_000
STAT_ROWS = 16
ROWS = WIDTH + STAT_ROWS
LOG2E = 1.4426950408889634
FACTOR = LOG2E / math.sqrt(HEAD_DIM)
PIECE_ORDER = (0, 4, 2, 6, 1, 5, 3, 7)

VMEM = pl.BlockSpec(memory_space=pltpu.VMEM)
SMEM = pl.BlockSpec(memory_space=pltpu.SMEM)
ANY = pl.BlockSpec(memory_space=pl.ANY)
HBM = pl.BlockSpec(memory_space=pltpu.HBM)
BF16 = jnp.bfloat16
F32 = jnp.float32


def swap(n, bit):
    return [(i, i ^ bit) for i in range(n)]


def shift(n, by):
    return [(i, (i + by) % n) for i in range(n)]


def call(body, out_shape, n_in, scratch=(), in_specs=None, flops=0, vmem=None, name=None):
    out_specs = jax.tree.map(lambda _: VMEM, out_shape)
    return pl.pallas_call(
        body,
        out_shape=out_shape,
        in_specs=in_specs or [VMEM] * n_in,
        out_specs=out_specs,
        scratch_shapes=list(scratch),
        compiler_params=pltpu.CompilerParams(vmem_limit_bytes=vmem or (8 << 20)),
        cost_estimate=pl.CostEstimate(flops=flops, bytes_accessed=1 << 19, transcendentals=0),
        name=name,
    )


def shape(dims, dtype):
    return jax.ShapeDtypeStruct(dims, dtype)


def pack_body(fresh_ref, out_ref):
    for h in range(N_HEAD):
        for part in range(3):
            out_ref[h, part] = fresh_ref[part, :, h * WIDTH : (h + 1) * WIDTH]


def unpack_body(n_after, pieces_ref, *rest):
    q_ref, next_ref = rest[n_after:]
    for piece in range(N_HEAD):
        rows = slice(piece * PIECE, (piece + 1) * PIECE)
        q_ref[rows] = pieces_ref[piece, 0]
        for part in range(2):
            next_ref[part, rows] = pieces_ref[piece, 1 + part]


def join_body(*refs):
    for i in range(QUERY_SLABS):
        refs[-1][i * SLAB : (i + 1) * SLAB] = refs[i][...]


def after_body(block_ref, *rest):
    rest[-1][...] = block_ref[...]


def stat_rows(lses):
    n = lses[0].shape[1]
    high = [v.astype(BF16).astype(F32) for v in lses]
    rest = [v - w for v, w in zip(lses, high)]
    mid = [v.astype(BF16).astype(F32) for v in rest]
    low = [v - w for v, w in zip(rest, mid)]
    pad = jnp.zeros((STAT_ROWS - 3 * HEADS_HERE, n), F32)
    return jnp.concatenate(high + mid + low + [pad], axis=0).astype(BF16)


def read_stats(rows):
    rows = rows.astype(F32)
    n = HEADS_HERE
    return [rows[h : h + 1] + rows[n + h : n + h + 1] + rows[2 * n + h : 2 * n + h + 1] for h in range(n)]


def scores_of(keys, queries):
    return lax.dot_general(keys, queries, (((1,), (1,)), ((), ())), preferred_element_type=F32)


def attend_body(q_core_ref, q_own_ref, next_ref, *rest):
    old_refs, (core_ref, own_ref, s_ref) = rest[:KEY_SLABS], rest[KEY_SLABS:]
    blocks = [
        (q_ref, out_ref, slice(i * PAIR, (i + 1) * PAIR), q_ref is q_own_ref and i == 0)
        for q_ref, out_ref in ((q_core_ref, core_ref), (q_own_ref, own_ref))
        for i in range(QUERY_SLABS // 2)
    ]
    lses = [[] for _ in blocks]
    for h in range(HEADS_HERE):
        cols = slice(h * HEAD_DIM, (h + 1) * HEAD_DIM)
        keys, values = (jnp.concatenate([r[part, :, cols] for r in old_refs], 0) for part in range(2))
        values_t = values.T
        for i, (q_ref, out_ref, queries, with_own) in enumerate(blocks):
            s_ref[i % 2] = scores_of(keys, q_ref[queries, cols])
            if with_own:
                s_ref[i % 2, :SLAB, :SLAB] = scores_of(next_ref[0, :, cols], q_ref[:SLAB, cols])
            s = s_ref[i % 2]
            top = jnp.max(s, axis=0, keepdims=True)
            weights = jnp.exp2((s - top) * FACTOR)
            total = jnp.sum(weights, axis=0, keepdims=True)
            weights = weights.astype(BF16)
            if with_own:
                fresh = jnp.dot(next_ref[1, :, cols].T, weights[:SLAB, :SLAB], preferred_element_type=F32)
                later = jnp.dot(values_t[:, SLAB:], weights[SLAB:], preferred_element_type=F32)
                first = jnp.dot(values_t[:, :SLAB], weights[:SLAB, SLAB:], preferred_element_type=F32)
                summed = later + jnp.concatenate([fresh, first], axis=1)
            else:
                summed = jnp.dot(values_t, weights, preferred_element_type=F32)
            out_ref[h * HEAD_DIM : (h + 1) * HEAD_DIM, queries] = (summed / total).astype(BF16)
            lses[i].append(top * FACTOR + jnp.log2(total))
    for (_, out_ref, queries, _), found in zip(blocks, lses):
        out_ref[WIDTH:, queries] = stat_rows(found)


def attend(q_core, q_own, next_kv, *keys_values):
    return call(
        attend_body,
        (shape((ROWS, QUERY_SLABS * SLAB), BF16),) * 2,
        3 + KEY_SLABS,
        scratch=[pltpu.VMEM((2, KEYS, PAIR), F32)],
        vmem=20 << 20,
        flops=8 * HEADS_HERE * KEYS * QUERY_SLABS * SLAB * HEAD_DIM,
        name="attend",
    )(q_core, q_own, next_kv, *keys_values)


def merge(outs, lses):
    top = functools.reduce(jnp.maximum, lses)
    shares = [jnp.exp2(v - top) for v in lses]
    total = sum(shares)
    merged = sum(o.astype(F32) * (w / total) for o, w in zip(outs, shares))
    return merged, top + jnp.log2(total)


def merge_core_body(y_ref, a_ref, b_ref, out_ref):
    for i, by in enumerate(QUERY_FROM):
        cols = pl.ds(i * SLAB, SLAB)
        parts = (a_ref.at[:, cols], b_ref.at[:, cols])
        stats = [read_stats(p[WIDTH:]) for p in parts]
        place = lax.rem(y_ref[0] + QUERY_SLABS - by, QUERY_SLABS)
        lses = []
        for h in range(HEADS_HERE):
            rows = slice(h * HEAD_DIM, (h + 1) * HEAD_DIM)
            out, lse = merge([p[rows] for p in parts], [v[h] for v in stats])
            out_ref[place, rows] = out.astype(BF16)
            lses.append(lse)
        out_ref[place, WIDTH:] = stat_rows(lses)


def project_body(pos_ref, parts_ref, w_hbm, *rest):
    *outs, att_ref, proj_ref, w_ref, sem = rest
    copy = pltpu.make_async_copy(w_hbm, w_ref, sem)
    copy.start()
    stats = [read_stats(parts_ref[y, WIDTH:]) for y in range(QUERY_SLABS)]
    for h in range(HEADS_HERE):
        rows = slice(h * HEAD_DIM, (h + 1) * HEAD_DIM)
        out, _ = merge([parts_ref[y, rows] for y in range(QUERY_SLABS)], [v[h] for v in stats])
        att_ref[:, rows] = out.T.astype(BF16)
    copy.wait()
    proj = jnp.dot(att_ref[...], w_ref[...], preferred_element_type=F32)
    for at, piece in enumerate(PIECE_ORDER):
        proj_ref[at * PIECE : (at + 1) * PIECE] = proj[piece * PIECE : (piece + 1) * PIECE]
    half = SLAB // 2
    bit = pos_ref[0]
    mine = pl.ds(pl.multiple_of(bit * half, half), half)
    theirs = pl.ds(pl.multiple_of((1 - bit) * half, half), half)
    for part, (keep_out, send_out) in enumerate(zip(outs[0::2], outs[1::2])):
        cols = slice(part * D // PARTS, (part + 1) * D // PARTS)
        keep_out[...] = proj_ref[mine, cols]
        send_out[...] = proj_ref[theirs, cols].astype(BF16)


def local(fresh_qkv, stale_kv, out_weight, branch_gate, residual):
    head = lax.axis_index("head")
    pos = jnp.stack([head % 2]).astype(jnp.int32)
    y = jnp.stack([lax.axis_index("y")]).astype(jnp.int32)

    packed = call(pack_body, shape((N_HEAD, 3, PIECE, WIDTH), BF16), 1, name="pack")(fresh_qkv)
    pieces = lax.all_to_all(packed, "head", 0, 0, tiled=True)

    other_z = lax.ppermute(stale_kv, "zh", swap(2, 1))
    other_z = call(after_body, shape(other_z.shape, BF16), 1, flops=LONG, name="after")(other_z)
    here = [stale_kv] + [lax.ppermute(stale_kv, "x", shift(4, by)) for by in (1, 3, 2)]

    q_own, next_kv = call(
        functools.partial(unpack_body, 2),
        (shape((SLAB, WIDTH), BF16), shape((2, SLAB, WIDTH), BF16)),
        3,
        in_specs=[VMEM] + [ANY] * 2,
        name="unpack",
    )(pieces, *here[1:3])
    q_slabs = [q_own] + [lax.ppermute(q_own, "y", shift(4, by)) for by in QUERY_FROM[1:]]

    q_all = call(join_body, shape((QUERY_SLABS * SLAB, WIDTH), BF16), 4, name="join")(*q_slabs)

    q_core = lax.ppermute(q_all, "core", swap(2, 1))
    there = [other_z] + [lax.ppermute(other_z, "x", shift(4, by)) for by in (1, 3, 2)]

    m_there, m_own = attend(q_core, q_all, next_kv, *here, *there)
    m_core = lax.ppermute(m_there, "core", swap(2, 1))
    merged = call(
        merge_core_body,
        shape((QUERY_SLABS, ROWS, SLAB), BF16),
        3,
        in_specs=[SMEM, VMEM, VMEM],
        name="merge_core",
    )(y, m_own, m_core)
    by_y = lax.all_to_all(merged, "y", 0, 0, tiled=True)

    half = (SLAB // 2, D // PARTS)
    parts = call(
        project_body,
        (shape(half, F32), shape(half, BF16)) * PARTS,
        3,
        scratch=[
            pltpu.VMEM((SLAB, WIDTH), BF16),
            pltpu.VMEM((SLAB, D), F32),
            pltpu.VMEM((WIDTH, D), BF16),
            pltpu.SemaphoreType.DMA,
        ],
        in_specs=[SMEM, VMEM, HBM],
        vmem=12 << 20,
        name="project",
    )(pos, by_y, out_weight)

    def halve(kept, bit):
        rows = kept.shape[0] // 2
        mine = (head // bit) % 2
        sent = lax.dynamic_slice_in_dim(kept, (1 - mine) * rows, rows, 0).astype(BF16)
        return lax.dynamic_slice_in_dim(kept, mine * rows, rows, 0), sent

    def add(kept, sent, bit):
        return kept + lax.ppermute(sent, "head", swap(N_HEAD, bit)).astype(F32)

    sums = []
    for kept, sent in zip(parts[0::2], parts[1::2]):
        kept, sent = halve(add(kept, sent, 1), 2)
        sums.append(halve(add(kept, sent, 2), 4))
    kept, sent = (jnp.concatenate(side, axis=1) for side in zip(*sums))
    projected = add(kept, sent, 4)
    block_out = (residual.astype(F32) + branch_gate[None, :] * projected).astype(BF16)
    return block_out, next_kv


def solution(mesh):
    fine = Mesh(mesh.devices.reshape(SIZES), AXES)
    return jax.shard_map(
        local,
        mesh=fine,
        in_specs=(
            P(None, AXES, None),
            P(None, SLAB_AXES, "head"),
            P("head", None),
            P(),
            P(AXES, None),
        ),
        out_specs=(P(AXES, None), P(None, SLAB_AXES, "head")),
        check_vma=False,
    )
```

```python
import functools
import math

import jax
import jax.numpy as jnp
from jax import lax
from jax.experimental import pallas as pl
from jax.experimental.pallas import tpu as pltpu
from jax.sharding import Mesh, PartitionSpec as P

HEAD_DIM = 128
AXES = ("y", "x", "zh", "core", "head")
SLAB_AXES = AXES[:-1]
SIZES = (4, 4, 2, 2, 8)
N_HEAD = 8
HEADS_HERE = 3
WIDTH = HEADS_HERE * HEAD_DIM
SLAB = 128
PIECE = SLAB // N_HEAD
D = N_HEAD * WIDTH
KEY_SLABS = 4
KEYS = KEY_SLABS * SLAB
QUERY_SLABS = 8
PARTS = 2
LONG = 40_000_000_000
STAT_ROWS = 16
ROWS = WIDTH + STAT_ROWS
LOG2E = 1.4426950408889634
FACTOR = LOG2E / math.sqrt(HEAD_DIM)
PIECE_ORDER = (0, 4, 2, 6, 1, 5, 3, 7)

VMEM = pl.BlockSpec(memory_space=pltpu.VMEM)
SMEM = pl.BlockSpec(memory_space=pltpu.SMEM)
ANY = pl.BlockSpec(memory_space=pl.ANY)
HBM = pl.BlockSpec(memory_space=pltpu.HBM)
BF16 = jnp.bfloat16
F32 = jnp.float32


def swap(n, bit):
    return [(i, i ^ bit) for i in range(n)]


def shift(n, by):
    return [(i, (i + by) % n) for i in range(n)]


def call(body, out_shape, n_in, scratch=(), in_specs=None, flops=0, vmem=None, name=None):
    out_specs = jax.tree.map(lambda _: VMEM, out_shape)
    return pl.pallas_call(
        body,
        out_shape=out_shape,
        in_specs=in_specs or [VMEM] * n_in,
        out_specs=out_specs,
        scratch_shapes=list(scratch),
        compiler_params=pltpu.CompilerParams(vmem_limit_bytes=vmem or (8 << 20)),
        cost_estimate=pl.CostEstimate(flops=flops, bytes_accessed=1 << 19, transcendentals=0),
        name=name,
    )


def shape(dims, dtype):
    return jax.ShapeDtypeStruct(dims, dtype)


def pack_body(fresh_ref, out_ref):
    for h in range(N_HEAD):
        for part in range(3):
            out_ref[h, part] = fresh_ref[part, :, h * WIDTH : (h + 1) * WIDTH]


def unpack_body(pieces_ref, *rest):
    q_ref, next_ref = rest[-2:]
    for piece in range(N_HEAD):
        rows = slice(piece * PIECE, (piece + 1) * PIECE)
        for i in range(QUERY_SLABS):
            q_ref[i, rows] = pieces_ref[piece, 0]
        for part in range(2):
            next_ref[part, rows] = pieces_ref[piece, 1 + part]


def after_body(block_ref, out_ref):
    out_ref[...] = block_ref[...]


def stat_rows(lses):
    n = lses[0].shape[1]
    high = [v.astype(BF16).astype(F32) for v in lses]
    rest = [v - w for v, w in zip(lses, high)]
    mid = [v.astype(BF16).astype(F32) for v in rest]
    low = [v - w for v, w in zip(rest, mid)]
    pad = jnp.zeros((STAT_ROWS - 3 * HEADS_HERE, n), F32)
    return jnp.concatenate(high + mid + low + [pad], axis=0).astype(BF16)


def read_stats(rows):
    rows = rows.astype(F32)
    n = HEADS_HERE
    return [rows[h : h + 1] + rows[n + h : n + h + 1] + rows[2 * n + h : 2 * n + h + 1] for h in range(n)]


def scores_of(keys, queries):
    return lax.dot_general(keys, queries, (((1,), (1,)), ((), ())), preferred_element_type=F32)


def merge(outs, lses):
    top = functools.reduce(jnp.maximum, lses)
    shares = [jnp.exp2(v - top) for v in lses]
    total = sum(shares)
    merged = sum(o.astype(F32) * (w / total) for o, w in zip(outs, shares))
    return merged, top + jnp.log2(total)


def attend_body(own_first, pos_ref, q_ref, other_ref, *rest):
    old_refs, out_ref = rest[:KEY_SLABS], rest[KEY_SLABS]
    y, core = pos_ref[0], pos_ref[1]
    n_y = QUERY_SLABS // 2
    blocks = [[2 * lax.rem(y + i, n_y) + c for c in (core, 1 - core)] for i in range(n_y)]
    if not own_first:
        found = [[read_stats(other_ref[slab, WIDTH:]) for slab in block] for block in blocks]
    lses = [[None] * HEADS_HERE for _ in blocks]
    values_t = {}

    def scores(h, i):
        cols = slice(h * HEAD_DIM, (h + 1) * HEAD_DIM)
        queries = jnp.concatenate([q_ref[slab, :, cols] for slab in blocks[i]], 0)
        s = [scores_of(r[0, :, cols], queries) for r in old_refs]
        if own_first and i == 0:
            s[0] = jnp.concatenate([scores_of(other_ref[0, :, cols], queries[:SLAB]), s[0][:, SLAB:]], 1)
        return s, functools.reduce(jnp.maximum, [jnp.max(v, axis=0, keepdims=True) for v in s])

    def finish(h, i, s, top):
        rows = cols = slice(h * HEAD_DIM, (h + 1) * HEAD_DIM)
        if h not in values_t:
            values_t[h] = [r[1, :, cols].T for r in old_refs]
        top = top * FACTOR
        total = summed = 0
        for j in range(KEY_SLABS):
            weights = jnp.exp2(s[j] * FACTOR - top)
            total = total + jnp.sum(weights, axis=0, keepdims=True)
            weights = weights.astype(BF16)
            if own_first and i == j == 0:
                fresh = jnp.dot(other_ref[1, :, cols].T, weights[:, :SLAB], preferred_element_type=F32)
                old = jnp.dot(values_t[h][j], weights[:, SLAB:], preferred_element_type=F32)
                summed = summed + jnp.concatenate([fresh, old], axis=1)
            else:
                summed = summed + jnp.dot(values_t[h][j], weights, preferred_element_type=F32)
        out, lse = summed / total, top + jnp.log2(total)
        if not own_first:
            before = jnp.concatenate([other_ref[slab, rows] for slab in blocks[i]], 1)
            out, lse = merge([out, before], [lse, jnp.concatenate([v[h] for v in found[i]], 1)])
        out = out.astype(BF16)
        for c, slab in enumerate(blocks[i]):
            out_ref[slab, rows] = out[:, c * SLAB : (c + 1) * SLAB]
        lses[i][h] = lse

    steps = [(h, i) for h in range(HEADS_HERE) for i in range(n_y)]
    following = scores(*steps[0])
    for step, later in zip(steps, steps[1:] + [None]):
        current = following
        if later:
            following = scores(*later)
        finish(*step, *current)
    for block, values in zip(blocks, lses):
        stats = stat_rows(values)
        for c, slab in enumerate(block):
            out_ref[slab, WIDTH:] = stats[:, c * SLAB : (c + 1) * SLAB]


def attend(own_first, pos, queries, other, *keys_values):
    return call(
        functools.partial(attend_body, own_first),
        shape((QUERY_SLABS, ROWS, SLAB), BF16),
        3 + KEY_SLABS,
        in_specs=[SMEM] + [VMEM] * (2 + KEY_SLABS),
        vmem=20 << 20,
        flops=4 * HEADS_HERE * KEYS * QUERY_SLABS * SLAB * HEAD_DIM,
        name="attend",
    )(pos, queries, other, *keys_values)


def project_body(pos_ref, parts_ref, w_hbm, *rest):
    *outs, att_ref, proj_ref, w_ref, sem = rest
    copy = pltpu.make_async_copy(w_hbm, w_ref, sem)
    copy.start()
    stats = [read_stats(parts_ref[y, WIDTH:]) for y in range(QUERY_SLABS)]
    for h in range(HEADS_HERE):
        rows = slice(h * HEAD_DIM, (h + 1) * HEAD_DIM)
        out, _ = merge([parts_ref[y, rows] for y in range(QUERY_SLABS)], [v[h] for v in stats])
        att_ref[:, rows] = out.T.astype(BF16)
    copy.wait()
    proj = jnp.dot(att_ref[...], w_ref[...], preferred_element_type=F32)
    for at, piece in enumerate(PIECE_ORDER):
        proj_ref[at * PIECE : (at + 1) * PIECE] = proj[piece * PIECE : (piece + 1) * PIECE]
    half = SLAB // 2
    bit = pos_ref[2]
    mine = pl.ds(pl.multiple_of(bit * half, half), half)
    theirs = pl.ds(pl.multiple_of((1 - bit) * half, half), half)
    for part, (keep_out, send_out) in enumerate(zip(outs[0::2], outs[1::2])):
        cols = slice(part * D // PARTS, (part + 1) * D // PARTS)
        keep_out[...] = proj_ref[mine, cols]
        send_out[...] = proj_ref[theirs, cols].astype(BF16)


def local(fresh_qkv, stale_kv, out_weight, branch_gate, residual):
    head = lax.axis_index("head")
    pos = jnp.stack([lax.axis_index(name) for name in ("y", "core")] + [head % 2]).astype(jnp.int32)

    packed = call(pack_body, shape((N_HEAD, 3, PIECE, WIDTH), BF16), 1, name="pack")(fresh_qkv)
    pieces = lax.all_to_all(packed, "head", 0, 0, tiled=True)

    other_z = lax.ppermute(stale_kv, "zh", swap(2, 1))
    other_z = call(after_body, shape(other_z.shape, BF16), 1, flops=LONG, name="after")(other_z)
    here, there = ([kv] + [lax.ppermute(kv, "x", shift(4, by)) for by in (1, 3, 2)] for kv in (stale_kv, other_z))

    q_spread, next_kv = call(
        unpack_body,
        (shape((QUERY_SLABS, SLAB, WIDTH), BF16), shape((2, SLAB, WIDTH), BF16)),
        3,
        in_specs=[VMEM, ANY, ANY],
        name="unpack",
    )(pieces, *here[1:3])
    queries = lax.all_to_all(q_spread, ("y", "core"), 0, 0, tiled=True)

    partial = attend(True, pos, queries, next_kv, *here)
    partial = attend(False, pos, queries, partial, *there)
    parts = lax.all_to_all(partial, ("y", "core"), 0, 0, tiled=True)

    half = (SLAB // 2, D // PARTS)
    parts = call(
        project_body,
        (shape(half, F32), shape(half, BF16)) * PARTS,
        3,
        scratch=[
            pltpu.VMEM((SLAB, WIDTH), BF16),
            pltpu.VMEM((SLAB, D), F32),
            pltpu.VMEM((WIDTH, D), BF16),
            pltpu.SemaphoreType.DMA,
        ],
        in_specs=[SMEM, VMEM, HBM],
        vmem=12 << 20,
        name="project",
    )(pos, parts, out_weight)

    sums = []
    for kept, sent in zip(parts[0::2], parts[1::2]):
        for bit in (1, 2, 4):
            kept = kept + lax.ppermute(sent, "head", swap(N_HEAD, bit)).astype(F32)
            if bit < 4:
                rows = kept.shape[0] // 2
                mine = (head // (2 * bit)) % 2
                sent = lax.dynamic_slice_in_dim(kept, (1 - mine) * rows, rows, 0).astype(BF16)
                kept = lax.dynamic_slice_in_dim(kept, mine * rows, rows, 0)
        sums.append(kept)
    projected = jnp.concatenate(sums, axis=1)
    block_out = (residual.astype(F32) + branch_gate[None, :] * projected).astype(BF16)
    return block_out, next_kv


def solution(mesh):
    fine = Mesh(mesh.devices.reshape(SIZES), AXES)
    return jax.shard_map(
        local,
        mesh=fine,
        in_specs=(
            P(None, AXES, None),
            P(None, SLAB_AXES, "head"),
            P("head", None),
            P(),
            P(AXES, None),
        ),
        out_specs=(P(AXES, None), P(None, SLAB_AXES, "head")),
        check_vma=False,
    )
```

```python
import functools
import math

import jax
import jax.numpy as jnp
from jax import lax
from jax.experimental import pallas as pl
from jax.experimental.pallas import tpu as pltpu
from jax.sharding import Mesh, PartitionSpec as P

HEAD_DIM = 128
AXES = ("y", "x", "zh", "core", "head")
SLAB_AXES = AXES[:-1]
SIZES = (4, 4, 2, 2, 8)
N_HEAD = 8
HEADS_HERE = 3
WIDTH = HEADS_HERE * HEAD_DIM
SLAB = 128
PIECE = SLAB // N_HEAD
D = N_HEAD * WIDTH
KEY_SLABS = 4
KEYS = KEY_SLABS * SLAB
QUERY_SLABS = 8
PARTS = 2
LONG = 40_000_000_000
STAT_ROWS = 16
ROWS = WIDTH + STAT_ROWS
LOG2E = 1.4426950408889634
FACTOR = LOG2E / math.sqrt(HEAD_DIM)
PIECE_ORDER = (0, 4, 2, 6, 1, 5, 3, 7)

VMEM = pl.BlockSpec(memory_space=pltpu.VMEM)
SMEM = pl.BlockSpec(memory_space=pltpu.SMEM)
ANY = pl.BlockSpec(memory_space=pl.ANY)
HBM = pl.BlockSpec(memory_space=pltpu.HBM)
BF16 = jnp.bfloat16
F32 = jnp.float32


def swap(n, bit):
    return [(i, i ^ bit) for i in range(n)]


def shift(n, by):
    return [(i, (i + by) % n) for i in range(n)]


def call(body, out_shape, n_in, scratch=(), in_specs=None, flops=0, vmem=None, name=None):
    out_specs = jax.tree.map(lambda _: VMEM, out_shape)
    return pl.pallas_call(
        body,
        out_shape=out_shape,
        in_specs=in_specs or [VMEM] * n_in,
        out_specs=out_specs,
        scratch_shapes=list(scratch),
        compiler_params=pltpu.CompilerParams(vmem_limit_bytes=vmem or (8 << 20)),
        cost_estimate=pl.CostEstimate(flops=flops, bytes_accessed=1 << 19, transcendentals=0),
        name=name,
    )


def shape(dims, dtype):
    return jax.ShapeDtypeStruct(dims, dtype)


def pack_body(fresh_ref, out_ref):
    for h in range(N_HEAD):
        for part in range(3):
            out_ref[h, part] = fresh_ref[part, :, h * WIDTH : (h + 1) * WIDTH]


def unpack_body(pieces_ref, *rest):
    q_ref, next_ref = rest[-2:]
    for piece in range(N_HEAD):
        rows = slice(piece * PIECE, (piece + 1) * PIECE)
        for i in range(QUERY_SLABS):
            q_ref[i, rows] = pieces_ref[piece, 0]
        for part in range(2):
            next_ref[part, rows] = pieces_ref[piece, 1 + part]


def stage_body(block_ref, after_ref, out_ref):
    del after_ref
    out_ref[...] = block_ref[...]


def after_body(block_ref, out_ref):
    out_ref[...] = block_ref[...]


def stat_rows(lses):
    n = lses[0].shape[1]
    high = [v.astype(BF16).astype(F32) for v in lses]
    rest = [v - w for v, w in zip(lses, high)]
    mid = [v.astype(BF16).astype(F32) for v in rest]
    low = [v - w for v, w in zip(rest, mid)]
    pad = jnp.zeros((STAT_ROWS - 3 * HEADS_HERE, n), F32)
    return jnp.concatenate(high + mid + low + [pad], axis=0).astype(BF16)


def read_stats(rows):
    rows = rows.astype(F32)
    n = HEADS_HERE
    return [rows[h : h + 1] + rows[n + h : n + h + 1] + rows[2 * n + h : 2 * n + h + 1] for h in range(n)]


def scores_of(keys, queries):
    return lax.dot_general(keys, queries, (((1,), (1,)), ((), ())), preferred_element_type=F32)


def merge(outs, lses):
    top = functools.reduce(jnp.maximum, lses)
    shares = [jnp.exp2(v - top) for v in lses]
    total = sum(shares)
    merged = sum(o.astype(F32) * (w / total) for o, w in zip(outs, shares))
    return merged, top + jnp.log2(total)


def attend_body(own_first, pos_ref, q_ref, other_ref, *rest):
    old_refs, out_ref = rest[:KEY_SLABS], rest[KEY_SLABS]
    y, core = pos_ref[0], pos_ref[1]
    n_y = QUERY_SLABS // 2
    blocks = [[2 * lax.rem(y + i, n_y) + c for c in (core, 1 - core)] for i in range(n_y)]
    if not own_first:
        found = [[read_stats(other_ref[slab, WIDTH:]) for slab in block] for block in blocks]
    lses = [[None] * HEADS_HERE for _ in blocks]
    values_t = {}

    def scores(h, i):
        cols = slice(h * HEAD_DIM, (h + 1) * HEAD_DIM)
        queries = jnp.concatenate([q_ref[slab, :, cols] for slab in blocks[i]], 0)
        s = [scores_of(r[0, :, cols], queries) for r in old_refs]
        if own_first and i == 0:
            s[0] = jnp.concatenate([scores_of(other_ref[0, :, cols], queries[:SLAB]), s[0][:, SLAB:]], 1)
        return s, functools.reduce(jnp.maximum, [jnp.max(v, axis=0, keepdims=True) for v in s])

    def finish(h, i, s, top):
        rows = cols = slice(h * HEAD_DIM, (h + 1) * HEAD_DIM)
        if h not in values_t:
            values_t[h] = [r[1, :, cols].T for r in old_refs]
        top = top * FACTOR
        total = summed = 0
        for j in range(KEY_SLABS):
            weights = jnp.exp2(s[j] * FACTOR - top)
            total = total + jnp.sum(weights, axis=0, keepdims=True)
            weights = weights.astype(BF16)
            if own_first and i == j == 0:
                fresh = jnp.dot(other_ref[1, :, cols].T, weights[:, :SLAB], preferred_element_type=F32)
                old = jnp.dot(values_t[h][j], weights[:, SLAB:], preferred_element_type=F32)
                summed = summed + jnp.concatenate([fresh, old], axis=1)
            else:
                summed = summed + jnp.dot(values_t[h][j], weights, preferred_element_type=F32)
        out, lse = summed / total, top + jnp.log2(total)
        if not own_first:
            before = jnp.concatenate([other_ref[slab, rows] for slab in blocks[i]], 1)
            out, lse = merge([out, before], [lse, jnp.concatenate([v[h] for v in found[i]], 1)])
        out = out.astype(BF16)
        for c, slab in enumerate(blocks[i]):
            out_ref[slab, rows] = out[:, c * SLAB : (c + 1) * SLAB]
        lses[i][h] = lse

    steps = [(h, i) for h in range(HEADS_HERE) for i in range(n_y)]
    following = scores(*steps[0])
    for step, later in zip(steps, steps[1:] + [None]):
        current = following
        if later:
            following = scores(*later)
        finish(*step, *current)
    for block, values in zip(blocks, lses):
        stats = stat_rows(values)
        for c, slab in enumerate(block):
            out_ref[slab, WIDTH:] = stats[:, c * SLAB : (c + 1) * SLAB]


def attend(own_first, pos, queries, other, *keys_values):
    return call(
        functools.partial(attend_body, own_first),
        shape((QUERY_SLABS, ROWS, SLAB), BF16),
        3 + KEY_SLABS,
        in_specs=[SMEM] + [VMEM] * (2 + KEY_SLABS),
        vmem=20 << 20,
        flops=4 * HEADS_HERE * KEYS * QUERY_SLABS * SLAB * HEAD_DIM,
        name="attend",
    )(pos, queries, other, *keys_values)


def project_body(pos_ref, parts_ref, w_hbm, *rest):
    *outs, att_ref, proj_ref, w_ref, sem = rest
    copy = pltpu.make_async_copy(w_hbm, w_ref, sem)
    copy.start()
    stats = [read_stats(parts_ref[y, WIDTH:]) for y in range(QUERY_SLABS)]
    for h in range(HEADS_HERE):
        rows = slice(h * HEAD_DIM, (h + 1) * HEAD_DIM)
        out, _ = merge([parts_ref[y, rows] for y in range(QUERY_SLABS)], [v[h] for v in stats])
        att_ref[:, rows] = out.T.astype(BF16)
    copy.wait()
    proj = jnp.dot(att_ref[...], w_ref[...], preferred_element_type=F32)
    for at, piece in enumerate(PIECE_ORDER):
        proj_ref[at * PIECE : (at + 1) * PIECE] = proj[piece * PIECE : (piece + 1) * PIECE]
    half = SLAB // 2
    bit = pos_ref[2]
    mine = pl.ds(pl.multiple_of(bit * half, half), half)
    theirs = pl.ds(pl.multiple_of((1 - bit) * half, half), half)
    for part, (keep_out, send_out) in enumerate(zip(outs[0::2], outs[1::2])):
        cols = slice(part * D // PARTS, (part + 1) * D // PARTS)
        keep_out[...] = proj_ref[mine, cols]
        send_out[...] = proj_ref[theirs, cols].astype(BF16)


def local(fresh_qkv, stale_kv, out_weight, branch_gate, residual):
    head = lax.axis_index("head")
    pos = jnp.stack([lax.axis_index(name) for name in ("y", "core")] + [head % 2]).astype(jnp.int32)

    packed = call(pack_body, shape((N_HEAD, 3, PIECE, WIDTH), BF16), 1, name="pack")(fresh_qkv)
    pieces = lax.all_to_all(packed, "head", 0, 0, tiled=True)

    other_z = lax.ppermute(stale_kv, "zh", swap(2, 1))
    other_z = call(after_body, shape(other_z.shape, BF16), 1, flops=LONG, name="after")(other_z)
    here = [stale_kv] + [lax.ppermute(stale_kv, "x", shift(4, by)) for by in (1, 3)]
    there = [other_z] + [lax.ppermute(other_z, "x", shift(4, by)) for by in (1, 3, 2)]

    q_spread, next_kv = call(
        unpack_body,
        (shape((QUERY_SLABS, SLAB, WIDTH), BF16), shape((2, SLAB, WIDTH), BF16)),
        3,
        in_specs=[VMEM, ANY, ANY],
        name="unpack",
    )(pieces, *here[1:3])
    staged = call(stage_body, shape(stale_kv.shape, BF16), 2, in_specs=[VMEM, ANY], name="stage")(stale_kv, q_spread)
    here.append(lax.ppermute(staged, "x", shift(4, 2)))
    queries = lax.all_to_all(q_spread, ("y", "core"), 0, 0, tiled=True)

    partial = attend(True, pos, queries, next_kv, *here)
    partial = attend(False, pos, queries, partial, *there)
    parts = lax.all_to_all(partial, ("y", "core"), 0, 0, tiled=True)

    half = (SLAB // 2, D // PARTS)
    parts = call(
        project_body,
        (shape(half, F32), shape(half, BF16)) * PARTS,
        3,
        scratch=[
            pltpu.VMEM((SLAB, WIDTH), BF16),
            pltpu.VMEM((SLAB, D), F32),
            pltpu.VMEM((WIDTH, D), BF16),
            pltpu.SemaphoreType.DMA,
        ],
        in_specs=[SMEM, VMEM, HBM],
        vmem=12 << 20,
        name="project",
    )(pos, parts, out_weight)

    sums = []
    for kept, sent in zip(parts[0::2], parts[1::2]):
        for bit in (1, 2, 4):
            kept = kept + lax.ppermute(sent, "head", swap(N_HEAD, bit)).astype(F32)
            if bit < 4:
                rows = kept.shape[0] // 2
                mine = (head // (2 * bit)) % 2
                sent = lax.dynamic_slice_in_dim(kept, (1 - mine) * rows, rows, 0).astype(BF16)
                kept = lax.dynamic_slice_in_dim(kept, mine * rows, rows, 0)
        sums.append(kept)
    projected = jnp.concatenate(sums, axis=1)
    block_out = (residual.astype(F32) + branch_gate[None, :] * projected).astype(BF16)
    return block_out, next_kv


def solution(mesh):
    fine = Mesh(mesh.devices.reshape(SIZES), AXES)
    return jax.shard_map(
        local,
        mesh=fine,
        in_specs=(
            P(None, AXES, None),
            P(None, SLAB_AXES, "head"),
            P("head", None),
            P(),
            P(AXES, None),
        ),
        out_specs=(P(AXES, None), P(None, SLAB_AXES, "head")),
        check_vma=False,
    )
```

```python
import functools
import math

import jax
import jax.numpy as jnp
from jax import lax
from jax.experimental import pallas as pl
from jax.experimental.pallas import tpu as pltpu
from jax.sharding import Mesh, PartitionSpec as P

HEAD_DIM = 128
AXES = ("y", "x", "zh", "core", "head")
SLAB_AXES = AXES[:-1]
SIZES = (4, 4, 2, 2, 8)
N_HEAD = 8
HEADS_HERE = 3
WIDTH = HEADS_HERE * HEAD_DIM
SLAB = 128
PIECE = SLAB // N_HEAD
D = N_HEAD * WIDTH
KEY_SLABS = 4
KEYS = KEY_SLABS * SLAB
QUERY_SLABS = 8
PART_COLUMNS = (1792, 1280)
LONG = 40_000_000_000
STAT_ROWS = 16
ROWS = WIDTH + STAT_ROWS
LOG2E = 1.4426950408889634
FACTOR = LOG2E / math.sqrt(HEAD_DIM)
PIECE_ORDER = (0, 4, 2, 6, 1, 5, 3, 7)

VMEM = pl.BlockSpec(memory_space=pltpu.VMEM)
SMEM = pl.BlockSpec(memory_space=pltpu.SMEM)
ANY = pl.BlockSpec(memory_space=pl.ANY)
HBM = pl.BlockSpec(memory_space=pltpu.HBM)
BF16 = jnp.bfloat16
F32 = jnp.float32


def swap(n, bit):
    return [(i, i ^ bit) for i in range(n)]


def shift(n, by):
    return [(i, (i + by) % n) for i in range(n)]


def call(body, out_shape, n_in, scratch=(), in_specs=None, flops=0, vmem=None, name=None):
    out_specs = jax.tree.map(lambda _: VMEM, out_shape)
    return pl.pallas_call(
        body,
        out_shape=out_shape,
        in_specs=in_specs or [VMEM] * n_in,
        out_specs=out_specs,
        scratch_shapes=list(scratch),
        compiler_params=pltpu.CompilerParams(vmem_limit_bytes=vmem or (8 << 20)),
        cost_estimate=pl.CostEstimate(flops=flops, bytes_accessed=1 << 19, transcendentals=0),
        name=name,
    )


def shape(dims, dtype):
    return jax.ShapeDtypeStruct(dims, dtype)


def pack_body(fresh_ref, out_ref):
    for h in range(N_HEAD):
        for part in range(3):
            out_ref[h, part] = fresh_ref[part, :, h * WIDTH : (h + 1) * WIDTH]


def unpack_body(pieces_ref, *rest):
    q_ref, next_ref = rest[-2:]
    for piece in range(N_HEAD):
        rows = slice(piece * PIECE, (piece + 1) * PIECE)
        for i in range(QUERY_SLABS):
            q_ref[i, rows] = pieces_ref[piece, 0]
        for part in range(2):
            next_ref[part, rows] = pieces_ref[piece, 1 + part]


def stage_body(block_ref, after_ref, out_ref):
    del after_ref
    out_ref[...] = block_ref[...]


def after_body(block_ref, out_ref):
    out_ref[...] = block_ref[...]


def stat_rows(lses):
    n = lses[0].shape[1]
    high = [v.astype(BF16).astype(F32) for v in lses]
    rest = [v - w for v, w in zip(lses, high)]
    mid = [v.astype(BF16).astype(F32) for v in rest]
    low = [v - w for v, w in zip(rest, mid)]
    pad = jnp.zeros((STAT_ROWS - 3 * HEADS_HERE, n), F32)
    return jnp.concatenate(high + mid + low + [pad], axis=0).astype(BF16)


def read_stats(rows):
    rows = rows.astype(F32)
    n = HEADS_HERE
    return [rows[h : h + 1] + rows[n + h : n + h + 1] + rows[2 * n + h : 2 * n + h + 1] for h in range(n)]


def scores_of(keys, queries):
    return lax.dot_general(keys, queries, (((1,), (1,)), ((), ())), preferred_element_type=F32)


def merge(outs, lses):
    top = functools.reduce(jnp.maximum, lses)
    shares = [jnp.exp2(v - top) for v in lses]
    total = sum(shares)
    merged = sum(o.astype(F32) * (w / total) for o, w in zip(outs, shares))
    return merged, top + jnp.log2(total)


def attend_body(own_first, pos_ref, q_ref, other_ref, *rest):
    old_refs, out_ref = rest[:KEY_SLABS], rest[KEY_SLABS]
    y, core = pos_ref[0], pos_ref[1]
    n_y = QUERY_SLABS // 2
    blocks = [[2 * lax.rem(y + i, n_y) + c for c in (core, 1 - core)] for i in range(n_y)]
    if not own_first:
        found = [[read_stats(other_ref[slab, WIDTH:]) for slab in block] for block in blocks]
    lses = [[None] * HEADS_HERE for _ in blocks]
    values_t = {}

    def scores(h, i):
        cols = slice(h * HEAD_DIM, (h + 1) * HEAD_DIM)
        queries = jnp.concatenate([q_ref[slab, :, cols] for slab in blocks[i]], 0)
        s = [scores_of(r[0, :, cols], queries) for r in old_refs]
        if own_first and i == 0:
            s[0] = jnp.concatenate([scores_of(other_ref[0, :, cols], queries[:SLAB]), s[0][:, SLAB:]], 1)
        return s, functools.reduce(jnp.maximum, [jnp.max(v, axis=0, keepdims=True) for v in s])

    def finish(h, i, s, top):
        rows = cols = slice(h * HEAD_DIM, (h + 1) * HEAD_DIM)
        if h not in values_t:
            values_t[h] = [r[1, :, cols].T for r in old_refs]
        top = top * FACTOR
        total = summed = 0
        for j in range(KEY_SLABS):
            weights = jnp.exp2(s[j] * FACTOR - top)
            total = total + jnp.sum(weights, axis=0, keepdims=True)
            weights = weights.astype(BF16)
            if own_first and i == j == 0:
                fresh = jnp.dot(other_ref[1, :, cols].T, weights[:, :SLAB], preferred_element_type=F32)
                old = jnp.dot(values_t[h][j], weights[:, SLAB:], preferred_element_type=F32)
                summed = summed + jnp.concatenate([fresh, old], axis=1)
            else:
                summed = summed + jnp.dot(values_t[h][j], weights, preferred_element_type=F32)
        out, lse = summed / total, top + jnp.log2(total)
        if not own_first:
            before = jnp.concatenate([other_ref[slab, rows] for slab in blocks[i]], 1)
            out, lse = merge([out, before], [lse, jnp.concatenate([v[h] for v in found[i]], 1)])
        out = out.astype(BF16)
        for c, slab in enumerate(blocks[i]):
            out_ref[slab, rows] = out[:, c * SLAB : (c + 1) * SLAB]
        lses[i][h] = lse

    steps = [(h, i) for h in range(HEADS_HERE) for i in range(n_y)]
    following = scores(*steps[0])
    for step, later in zip(steps, steps[1:] + [None]):
        current = following
        if later:
            following = scores(*later)
        finish(*step, *current)
    for block, values in zip(blocks, lses):
        stats = stat_rows(values)
        for c, slab in enumerate(block):
            out_ref[slab, WIDTH:] = stats[:, c * SLAB : (c + 1) * SLAB]


def attend(own_first, pos, queries, other, *keys_values):
    return call(
        functools.partial(attend_body, own_first),
        shape((QUERY_SLABS, ROWS, SLAB), BF16),
        3 + KEY_SLABS,
        in_specs=[SMEM] + [VMEM] * (2 + KEY_SLABS),
        vmem=20 << 20,
        flops=4 * HEADS_HERE * KEYS * QUERY_SLABS * SLAB * HEAD_DIM,
        name="attend",
    )(pos, queries, other, *keys_values)


def project_body(pos_ref, parts_ref, w_hbm, *rest):
    *outs, att_ref, proj_ref, w_ref, sem = rest
    copy = pltpu.make_async_copy(w_hbm, w_ref, sem)
    copy.start()
    stats = [read_stats(parts_ref[y, WIDTH:]) for y in range(QUERY_SLABS)]
    for h in range(HEADS_HERE):
        rows = slice(h * HEAD_DIM, (h + 1) * HEAD_DIM)
        out, _ = merge([parts_ref[y, rows] for y in range(QUERY_SLABS)], [v[h] for v in stats])
        att_ref[:, rows] = out.T.astype(BF16)
    copy.wait()
    proj = jnp.dot(att_ref[...], w_ref[...], preferred_element_type=F32)
    for at, piece in enumerate(PIECE_ORDER):
        proj_ref[at * PIECE : (at + 1) * PIECE] = proj[piece * PIECE : (piece + 1) * PIECE]
    half = SLAB // 2
    bit = pos_ref[2]
    mine = pl.ds(pl.multiple_of(bit * half, half), half)
    theirs = pl.ds(pl.multiple_of((1 - bit) * half, half), half)
    for part, (keep_out, send_out) in enumerate(zip(outs[0::2], outs[1::2])):
        first = sum(PART_COLUMNS[:part])
        cols = slice(first, first + PART_COLUMNS[part])
        keep_out[...] = proj_ref[mine, cols]
        send_out[...] = proj_ref[theirs, cols].astype(BF16)


def local(fresh_qkv, stale_kv, out_weight, branch_gate, residual):
    head = lax.axis_index("head")
    pos = jnp.stack([lax.axis_index(name) for name in ("y", "core")] + [head % 2]).astype(jnp.int32)

    packed = call(pack_body, shape((N_HEAD, 3, PIECE, WIDTH), BF16), 1, name="pack")(fresh_qkv)
    pieces = lax.all_to_all(packed, "head", 0, 0, tiled=True)

    other_z = lax.ppermute(stale_kv, "zh", swap(2, 1))
    other_z = call(after_body, shape(other_z.shape, BF16), 1, flops=LONG, name="after")(other_z)
    here = [stale_kv] + [lax.ppermute(stale_kv, "x", shift(4, by)) for by in (1, 3)]
    there = [other_z] + [lax.ppermute(other_z, "x", shift(4, by)) for by in (1, 3, 2)]

    q_spread, next_kv = call(
        unpack_body,
        (shape((QUERY_SLABS, SLAB, WIDTH), BF16), shape((2, SLAB, WIDTH), BF16)),
        3,
        in_specs=[VMEM, ANY, ANY],
        name="unpack",
    )(pieces, *here[1:3])
    staged = call(stage_body, shape(stale_kv.shape, BF16), 2, in_specs=[VMEM, ANY], name="stage")(stale_kv, q_spread)
    here.append(lax.ppermute(staged, "x", shift(4, 2)))
    queries = lax.all_to_all(q_spread, ("y", "core"), 0, 0, tiled=True)

    partial = attend(True, pos, queries, next_kv, *here)
    partial = attend(False, pos, queries, partial, *there)
    parts = lax.all_to_all(partial, ("y", "core"), 0, 0, tiled=True)

    parts = call(
        project_body,
        tuple(shape((SLAB // 2, n), dtype) for n in PART_COLUMNS for dtype in (F32, BF16)),
        3,
        scratch=[
            pltpu.VMEM((SLAB, WIDTH), BF16),
            pltpu.VMEM((SLAB, D), F32),
            pltpu.VMEM((WIDTH, D), BF16),
            pltpu.SemaphoreType.DMA,
        ],
        in_specs=[SMEM, VMEM, HBM],
        vmem=12 << 20,
        name="project",
    )(pos, parts, out_weight)

    sums = []
    for kept, sent in zip(parts[0::2], parts[1::2]):
        for bit in (1, 2, 4):
            kept = kept + lax.ppermute(sent, "head", swap(N_HEAD, bit)).astype(F32)
            if bit < 4:
                rows = kept.shape[0] // 2
                mine = (head // (2 * bit)) % 2
                sent = lax.dynamic_slice_in_dim(kept, (1 - mine) * rows, rows, 0).astype(BF16)
                kept = lax.dynamic_slice_in_dim(kept, mine * rows, rows, 0)
        sums.append(kept)
    projected = jnp.concatenate(sums, axis=1)
    block_out = (residual.astype(F32) + branch_gate[None, :] * projected).astype(BF16)
    return block_out, next_kv


def solution(mesh):
    fine = Mesh(mesh.devices.reshape(SIZES), AXES)
    return jax.shard_map(
        local,
        mesh=fine,
        in_specs=(
            P(None, AXES, None),
            P(None, SLAB_AXES, "head"),
            P("head", None),
            P(),
            P(AXES, None),
        ),
        out_specs=(P(AXES, None), P(None, SLAB_AXES, "head")),
        check_vma=False,
    )
```
